256 devices in a mesh: chan: 64 (over x, z, core), tm: 4 (over y).
Axes of the slice: x: 4, y: 4, z: 8, core: 2. Of those that a mesh axis runs over, the one named last changes fastest.
Arguments:
- voltages: bfloat16 [2, 128, 512, 8192], P(None, 'chan', None, 'tm'), may hold values from -6 to 6
- weights: bfloat16 [2, 128, 512, 512], P(None, 'chan'), may hold values from -0.1875 to 0.1875
- baseline: float32 [128, 512], P(None, 'chan'), may hold values from 28 to 36
- gains: float32 [128, 512], P(None, 'chan'), may hold values from 0.02 to 0.2
- offsets: int32 [128], replicated, may hold values from 0 to 4, as said below
- shifts: int32 [4, 128], replicated, may hold values from 0 to 8, as said below
- delays: int32 [8, 8], replicated, may hold values from 0 to 12, as said below
Outputs:
- dedispersed: float32 [128, 512, 512], P(None, 'chan', 'tm')
The draws below stay inside these ranges and needn't reach their ends.
Inputs may be any that keep to these rules, and one draw needn't show every extreme that they name: `offsets`: the largest value is reached in every draw. In section s the shifts are at most 2 ** s, and each section has a row at that bound. `delays`: the largest value is reached in every draw.
All inputs are finite; a program needn't handle non-finite values.
Results may differ from the reference program's by a relative error of at most 0.0011.
Values may be sent and summed in bfloat16 or wider, within the bound.
No kernel may reach another device: no remote copies, remote signals or barrier semaphores. Data moves between devices by JAX's collectives and lax.ppermute only.
A program may use at most 256 MiB of HBM per device.

```python
import math
import jax
import jax.numpy as jnp
from jax import lax

FEEDS = 512
BEAMS = 512
BIN = 16
LEVELS = 4
COARSE = 8
OFFMAX = 4
GMAX = 12
NCH = 128
NT = 8192
NTW = 512
TAIL = 31
GROUPS = 8


def draw_offsets(key, part):
    key = jax.random.fold_in(key, 11)
    first_key, second_key = jax.random.split(key)
    values = jax.random.randint(first_key, (NCH,), 0, OFFMAX + 1)
    chosen = jax.random.randint(second_key, (), 0, NCH)
    values = jnp.where(jnp.arange(NCH) == chosen, OFFMAX, values)
    return values.astype(jnp.int32)


def draw_shifts(key, part):
    key = jax.random.fold_in(key, 23)
    first_key, second_key = jax.random.split(key)
    bounds = (2 ** jnp.arange(LEVELS, dtype=jnp.int32)).reshape(LEVELS, 1)
    values = jax.random.randint(first_key, (LEVELS, NCH), 0, bounds + 1)
    chosen = jax.random.randint(second_key, (LEVELS, 1), 0, NCH)
    values = jnp.where(jnp.arange(NCH).reshape(1, NCH) == chosen, bounds, values)
    return values.astype(jnp.int32)


def draw_delays(key, part):
    key = jax.random.fold_in(key, 37)
    first_key, second_key = jax.random.split(key)
    values = jax.random.randint(first_key, (COARSE, GROUPS), 0, GMAX + 1)
    chosen = jax.random.randint(second_key, (), 0, COARSE * GROUPS)
    values = jnp.where(jnp.arange(COARSE * GROUPS).reshape(COARSE, GROUPS) == chosen, GMAX, values)
    return values.astype(jnp.int32)


def shard_levels(rng, dims, cuts, least, top_value):
    def one(dim, parts):
        heights = jax.random.uniform(jax.random.fold_in(jax.random.fold_in(rng, 6), dim), (parts,), jnp.float32, least / len(cuts), top_value / len(cuts))
        return jnp.repeat(jnp.exp(heights), dims[dim] // parts).reshape((-1,) + (1,) * (len(dims) - dim - 1))

    loudness = one(*cuts[0])
    for cut in cuts[1:]:
        loudness = loudness * one(*cut)
    return loudness


def gaussian(own_key, dims, deviation, reach, pieces=(), held_as=jnp.bfloat16):
    factor_of = shard_levels(own_key, dims, pieces, -0.22, 0.18) if pieces else 1.0
    array = jax.random.normal(own_key, dims, jnp.float32) * deviation * factor_of
    return jnp.minimum(jnp.maximum(array, -reach), reach).astype(held_as)


def setup_inputs(seed: int = 0) -> dict:
    key_list = jax.random.split(jax.random.key(seed), 8)
    voltages = gaussian(key_list[0], (2, NCH, FEEDS, NT), 1.0, 6.0, ((1, 64), (3, 4)))
    weights = gaussian(key_list[1], (2, NCH, BEAMS, FEEDS), (2 * FEEDS) ** -0.5, 0.1875, ((1, 64),))
    baseline = jnp.clip(28.0 + 8.0 * jax.random.uniform(key_list[2], (NCH, BEAMS), jnp.float32) ** shard_levels(key_list[2], (NCH, BEAMS), ((1, 64),), -0.2, 0.2), 28.0, 36.0)
    gains = jnp.clip(jnp.exp(math.log(0.2) - 2.3025851 * jax.random.uniform(key_list[3], (NCH, BEAMS), jnp.float32) ** shard_levels(key_list[3], (NCH, BEAMS), ((1, 64),), -0.2, 0.2)), 0.02, 0.2)
    offsets = draw_offsets(jax.random.fold_in(key_list[7], 71), 0)
    shifts = draw_shifts(jax.random.fold_in(key_list[7], 71), 0)
    delays = draw_delays(jax.random.fold_in(key_list[7], 71), 0)
    return {"voltages": voltages, "weights": weights, "baseline": baseline, "gains": gains, "offsets": offsets, "shifts": shifts, "delays": delays}


def dedisperse(series, offsets, shifts, delays, out_len):
    channels, beams_here, padded_len = series.shape
    start_len = padded_len - OFFMAX
    current = jax.vmap(lambda series_row, start_at: lax.dynamic_slice_in_dim(series_row, start_at, start_len, 1))(series, offsets).astype(jnp.float32)
    for level_idx in range(LEVELS):
        half_size = 2 ** level_idx
        cur_len = current.shape[2]
        new_len = cur_len - half_size
        blocks = current.reshape(channels // (2 * half_size), 2, half_size, beams_here, cur_len)
        lower_rows = jnp.repeat(blocks[:, 0], 2, axis=1).reshape(channels, beams_here, cur_len)
        upper_rows = jnp.repeat(blocks[:, 1], 2, axis=1).reshape(channels, beams_here, cur_len)
        shifted = jax.vmap(lambda series_row, start_at: lax.dynamic_slice_in_dim(series_row, start_at, new_len, 1))(upper_rows, shifts[level_idx])
        current = lower_rows[:, :, :new_len] + shifted
    tree_rows = 2 ** LEVELS
    grouped = current.reshape(channels // tree_rows, tree_rows, beams_here, current.shape[2])

    def coarse_trial(lag_row):
        aligned = jax.vmap(lambda group_block, start_at: lax.dynamic_slice_in_dim(group_block, start_at, out_len, 2))(grouped, lag_row)
        return jnp.sum(aligned, axis=0)

    summed = lax.map(coarse_trial, delays)
    return summed.reshape(delays.shape[0] * tree_rows, beams_here, out_len)


def reference(voltages, weights, baseline, gains, offsets, shifts, delays):
    def one_channel(channel):
        volt_block = lax.dynamic_index_in_dim(voltages, channel, 1, keepdims=False)
        weight_block = lax.dynamic_index_in_dim(weights, channel, 1, keepdims=False)
        real_part = jnp.dot(weight_block[0], volt_block[0], preferred_element_type=jnp.float32) - jnp.dot(weight_block[1], volt_block[1], preferred_element_type=jnp.float32)
        imag_part = jnp.dot(weight_block[0], volt_block[1], preferred_element_type=jnp.float32) + jnp.dot(weight_block[1], volt_block[0], preferred_element_type=jnp.float32)
        detected = real_part * real_part + imag_part * imag_part
        binned = jnp.sum(detected.reshape(BEAMS, NTW, BIN), axis=2)
        base_row = lax.dynamic_index_in_dim(baseline, channel, 0, keepdims=False)
        gain_row = lax.dynamic_index_in_dim(gains, channel, 0, keepdims=False)
        return ((binned - base_row[:, None]) * gain_row[:, None]).astype(jnp.bfloat16)

    normalized = lax.map(one_channel, jnp.arange(NCH, dtype=jnp.int32))
    padded = jnp.pad(normalized, ((0, 0), (0, 0), (0, TAIL)))
    return dedisperse(padded, offsets, shifts, delays, NTW)
```

```python
import functools
import jax
import jax.numpy as jnp
from jax import lax
from jax.experimental import pallas as pl
from jax.experimental.pallas import tpu as pltpu
from jax.sharding import PartitionSpec as P

LANES = 128
F32 = jnp.float32
BF16 = jnp.bfloat16
BIN = 16


def roll_lanes(x, steps):
    return pltpu.roll(x, steps % LANES, 1)


def fold_pair(a, b, stride):
    lane = lax.broadcasted_iota(jnp.int32, a.shape, 1)
    upper = (lane & stride) != 0
    return jnp.where(upper, b + roll_lanes(b, stride), a + roll_lanes(a, -stride))


def fold(tiles, stride):
    while len(tiles) > 1:
        tiles = [fold_pair(tiles[i], tiles[i + 1], stride) for i in range(0, len(tiles), 2)]
        stride *= 2
    return tiles[0]


def beamform_kernel(rows, v_ref, w_ref, out_ref, stacked, part, binned):
    channel, step = pl.program_id(0), pl.program_id(1)
    steps = pl.num_programs(1)
    beams, feeds = w_ref.shape[2:]
    width = v_ref.shape[3]

    @pl.when(step == 0)
    def _():
        for r in range(beams // rows):
            lo = 2 * r * rows
            src = pl.ds(r * rows, rows)
            stacked[lo : lo + rows, :feeds] = w_ref[0, 0, src, :]
            stacked[lo : lo + rows, feeds:] = -w_ref[1, 0, src, :]
            stacked[lo + rows : lo + 2 * rows, :feeds] = w_ref[1, 0, src, :]
            stacked[lo + rows : lo + 2 * rows, feeds:] = w_ref[0, 0, src, :]

    volts = v_ref[...].reshape(2 * feeds, width)
    for r in range(beams // rows):
        lo = 2 * r * rows
        both = jnp.dot(stacked[lo : lo + 2 * rows, :], volts, preferred_element_type=F32)
        real, imag = both[:rows], both[rows:]
        power = real * real + imag * imag
        tiles = [power[:, i : i + LANES] for i in range(0, width, LANES)]
        part[step, r * rows : (r + 1) * rows, :] = fold(tiles, 1)

    @pl.when(step == steps - 1)
    def _():
        count = 4
        stride = width // LANES
        total = fold([part[i] for i in range(count)], stride)
        lane = lax.broadcasted_iota(jnp.int32, total.shape, 1)
        source = ((lane & 7) << 4) | (lane >> 3)
        total = jnp.take_along_axis(total, source, axis=1)
        out_ref[:, pl.ds(pl.multiple_of(channel * 8, 8), 8), :] = total.reshape(beams // 8, 8, LANES)


def beamform(voltages, weights, rows=256, width=512):
    _, channels, feeds, samples = voltages.shape
    beams = weights.shape[2]
    steps = samples // width
    return pl.pallas_call(
        functools.partial(beamform_kernel, rows),
        grid=(channels, steps),
        in_specs=[
            pl.BlockSpec((2, 1, feeds, width), lambda c, i: (0, c, 0, i)),
            pl.BlockSpec((2, 1, beams, feeds), lambda c, i: (0, c, 0, 0)),
        ],
        out_specs=pl.BlockSpec((beams // 8, 8 * channels, LANES), lambda c, i: (0, 0, 0)),
        out_shape=jax.ShapeDtypeStruct((beams // 8, 8 * channels, LANES), F32),
        scratch_shapes=[
            pltpu.VMEM((2 * beams, 2 * feeds), BF16),
            pltpu.VMEM((steps, beams, LANES), F32),
            pltpu.VMEM((8, LANES), F32),
        ],
        compiler_params=pltpu.CompilerParams(
            dimension_semantics=("arbitrary", "arbitrary"), vmem_limit_bytes=48 * 1024 * 1024
        ),
    )(voltages, weights)


LEVELS = 4
TREE = 16
TAPS = 32
VMEM = 48 * 1024 * 1024


def taps_kernel(offsets_ref, shifts_ref, delays_ref, taps_ref):
    rows = lax.broadcasted_iota(jnp.int32, (LANES, LANES), 0)
    cols = lax.broadcasted_iota(jnp.int32, (LANES, LANES), 1)
    tree_row = rows & (TREE - 1)
    delay = jnp.broadcast_to(offsets_ref[...], (LANES, LANES)).astype(F32)
    for level in range(LEVELS):
        half = 2**level
        block = 2 * half
        here = (cols & (block - 1)) == (tree_row >> (LEVELS - 1 - level))
        held = jnp.where(here, shifts_ref[level : level + 1, :], 0).astype(F32).astype(BF16)
        reach = ((rows >> (level + 1)) == (cols >> (level + 1))) & ((cols & half) != 0)
        delay += jnp.dot(held, jnp.where(reach, 1.0, 0.0).astype(BF16), preferred_element_type=F32)
    groups = delays_ref.shape[1]
    row8 = lax.broadcasted_iota(jnp.int32, (groups, LANES), 0)
    col8 = lax.broadcasted_iota(jnp.int32, (groups, LANES), 1)
    of_group = jnp.where(row8 == (col8 >> LEVELS), 1.0, 0.0).astype(BF16)
    spread = jnp.dot(
        delays_ref[...].astype(F32).astype(BF16), of_group, preferred_element_type=F32
    )
    delay = delay.reshape(groups, TREE, LANES) + spread.reshape(groups, 1, LANES)
    delay = delay.reshape(LANES, LANES).astype(jnp.int32)
    for d in range(TAPS):
        taps_ref[:, d * LANES : (d + 1) * LANES] = jnp.where(delay == d, 1.0, 0.0).astype(BF16)


def make_taps(offsets, shifts, delays):
    return pl.pallas_call(
        taps_kernel,
        out_shape=jax.ShapeDtypeStruct((LANES, TAPS * LANES), BF16),
        cost_estimate=pl.CostEstimate(flops=4_000_000, bytes_accessed=1_100_000, transcendentals=0),
    )(offsets.reshape(1, LANES), shifts, delays)


def normalize(x, baseline_ref, gains_ref, b):
    return ((x - baseline_ref[:, b : b + 1]) * gains_ref[:, b : b + 1]).astype(BF16)


def own_kernel(taps_ref, binned_ref, baseline_ref, gains_ref, out_ref, *windows):
    beams = baseline_ref.shape[1]
    lane = lax.broadcasted_iota(jnp.int32, (LANES, LANES), 1)
    for pair in range(beams // 2):
        window = windows[pair % len(windows)]
        for j in range(2):
            b = 2 * pair + j
            x = normalize(binned_ref[pl.ds(b, LANES, stride=beams), :], baseline_ref, gains_ref, b)
            x = x.astype(F32)
            for d in range(TAPS):
                moved = x if d == 0 else jnp.where(lane < LANES - d, pltpu.roll(x, LANES - d, 1), 0.0)
                window[d * LANES : (d + 1) * LANES, j * LANES : (j + 1) * LANES] = moved.astype(BF16)
        both = jnp.dot(taps_ref[...], window[...], preferred_element_type=F32)
        for j in range(2):
            out_ref[pl.ds(2 * pair + j, LANES, stride=beams), :] = both[:, j * LANES : (j + 1) * LANES]


def dedisperse_own(taps, binned, baseline, gains):
    beams = baseline.shape[1]
    return pl.pallas_call(
        own_kernel,
        out_shape=jax.ShapeDtypeStruct((LANES * beams, LANES), F32),
        scratch_shapes=[pltpu.VMEM((TAPS * LANES, 2 * LANES), BF16)] * 2,
        compiler_params=pltpu.CompilerParams(vmem_limit_bytes=VMEM),
        cost_estimate=pl.CostEstimate(flops=4_000_000_000, bytes_accessed=3_000_000, transcendentals=0),
    )(taps, binned, baseline, gains)


def tail_kernel(taps_ref, tail_ref, baseline_ref, gains_ref, own_ref, out_ref, window):
    beams = baseline_ref.shape[1]
    per = LANES // TAPS
    lane = lax.broadcasted_iota(jnp.int32, (LANES, LANES), 1)
    for j in range(beams // per):
        x = jnp.concatenate(
            [
                normalize(tail_ref[pl.ds(b, LANES, stride=beams), :], baseline_ref, gains_ref, b).astype(F32)
                for b in range(j * per, (j + 1) * per)
            ],
            axis=1,
        )
        for d in range(TAPS):
            keep = (lane & (TAPS - 1)) >= TAPS - d
            moved = jnp.where(keep, pltpu.roll(x, (TAPS - d) % LANES, 1), 0.0)
            window[d * LANES : (d + 1) * LANES, j * LANES : (j + 1) * LANES] = moved.astype(BF16)
    added = jnp.dot(taps_ref[...], window[...], preferred_element_type=F32)
    for b in range(beams):
        rows = pl.ds(b, LANES, stride=beams)
        own = own_ref[rows, :]
        piece = added[:, b * TAPS : (b + 1) * TAPS]
        full = jnp.concatenate([jnp.zeros((LANES, LANES - TAPS), F32), piece], axis=1)
        out_ref[rows, :] = own + full


def add_tail(taps, tail, baseline, gains, own):
    beams = baseline.shape[1]
    return pl.pallas_call(
        tail_kernel,
        out_shape=jax.ShapeDtypeStruct((LANES * beams, LANES), F32),
        scratch_shapes=[pltpu.VMEM((TAPS * LANES, 2 * LANES), BF16)],
        compiler_params=pltpu.CompilerParams(vmem_limit_bytes=VMEM),
        input_output_aliases={4: 0},
        cost_estimate=pl.CostEstimate(flops=1_000_000_000, bytes_accessed=2_000_000, transcendentals=0),
    )(taps, tail, baseline, gains, own)


def from_behind(value, axis):
    count = lax.axis_size(axis)
    return lax.ppermute(value, axis, [(source, source - 1) for source in range(1, count)])


def per_device(voltages, weights, baseline, gains, offsets, shifts, delays):
    binned = beamform(voltages, weights)
    regrouped = lax.all_to_all(binned, "chan", split_axis=0, concat_axis=0, tiled=True)
    taps = make_taps(offsets, shifts, delays)
    channels, beams = baseline.shape
    regrouped = regrouped.reshape(channels * beams, LANES)
    following = from_behind(regrouped[:, :TAPS], "tm")
    inside = (lax.axis_index("tm") < lax.axis_size("tm") - 1).astype(F32)
    own = dedisperse_own(taps, regrouped, baseline, gains)
    full = add_tail(taps, following, baseline, gains * inside, own)
    return full.reshape(channels, beams, LANES)


def solution(mesh):
    placed = (
        P(None, "chan", None, "tm"),
        P(None, "chan", None, None),
        P(None, "chan"),
        P(None, "chan"),
        P(),
        P(),
        P(),
    )
    return jax.shard_map(
        per_device, mesh=mesh, in_specs=placed, out_specs=P(None, "chan", "tm"), check_vma=False
    )
```

```python
import functools
import jax
import jax.numpy as jnp
from jax import lax
from jax.experimental import pallas as pl
from jax.experimental.pallas import tpu as pltpu
from jax.sharding import PartitionSpec as P

LANES = 128
F32 = jnp.float32
BF16 = jnp.bfloat16
def fold_pair(a, b, stride):
    lane = lax.broadcasted_iota(jnp.int32, a.shape, 1)
    upper = (lane & stride) != 0
    return jnp.where(
        upper, b + pltpu.roll(b, stride, 1), a + pltpu.roll(a, LANES - stride, 1)
    )


def fold(tiles, stride):
    while len(tiles) > 1:
        tiles = [fold_pair(tiles[i], tiles[i + 1], stride) for i in range(0, len(tiles), 2)]
        stride *= 2
    return tiles[0]


def beamform_kernel(chunk, width, late, v_hbm, w_hbm, out_ref, volts, weights, part, sem):
    channels, feeds, samples = v_hbm.shape[1:]
    beams = w_hbm.shape[2]
    steps = samples // width
    copies = {}
    count = 0
    for c in range(channels):
        copies[c, "w"] = pltpu.make_async_copy(w_hbm.at[:, c], weights.at[:, c], sem.at[count])
        count += 1
        if c == 0:
            for i in range(steps):
                here = pl.ds(i * width, width)
                copies[c, i] = pltpu.make_async_copy(v_hbm.at[:, c, :, here], volts.at[:, c, :, here], sem.at[count])
                count += 1
        else:
            copies[c, 0] = pltpu.make_async_copy(v_hbm.at[:, c], volts.at[:, c], sem.at[count])
            count += 1
    for copy in copies.values():
        copy.start()

    lane = lax.broadcasted_iota(jnp.int32, (chunk, LANES), 1)
    source = ((lane & 7) << 4) | (lane >> 3)

    def detect(c, i, r, both):
        real, imag = both[:chunk], both[chunk:]
        power = real * real + imag * imag
        piece = fold([power[:, k : k + LANES] for k in range(0, width, LANES)], 1)
        if i < steps - 1:
            part[i, r : r + chunk, :] = piece
            return
        tiles = [part[k, r : r + chunk, :] for k in range(steps - 1)] + [piece]
        total = jnp.take_along_axis(fold(tiles, width // LANES), source, axis=1)
        out_ref[r // 8 : (r + chunk) // 8, 8 * c : 8 * c + 8, :] = total.reshape(chunk // 8, 8, LANES)

    waiting = []
    for c in range(channels):
        copies[c, "w"].wait()
        for i in range(steps):
            if (c, i) in copies:
                copies[c, i].wait()
            right = volts[:, c, :, i * width : (i + 1) * width].reshape(2 * feeds, width)
            for r in range(0, beams, chunk):
                w0, w1 = weights[0, c, r : r + chunk, :], weights[1, c, r : r + chunk, :]
                left = jnp.concatenate(
                    [jnp.concatenate([w0, -w1], axis=1), jnp.concatenate([w1, w0], axis=1)], axis=0
                )
                both = jnp.dot(left, right, preferred_element_type=F32)
                waiting.append((c, i, r, both))
                if len(waiting) > late:
                    detect(*waiting.pop(0))
    for item in waiting:
        detect(*item)


def beamform(voltages, weights, chunk=256, width=512, late=1):
    _, channels, feeds, samples = voltages.shape
    beams = weights.shape[2]
    return pl.pallas_call(
        functools.partial(beamform_kernel, chunk, width, late),
        in_specs=[pl.BlockSpec(memory_space=pl.ANY)] * 2,
        out_shape=jax.ShapeDtypeStruct((beams // 8, 8 * channels, LANES), F32),
        scratch_shapes=[
            pltpu.VMEM(voltages.shape, BF16),
            pltpu.VMEM(weights.shape, BF16),
            pltpu.VMEM((samples // width - 1, beams, LANES), F32),
            pltpu.SemaphoreType.DMA((16,)),
        ],
        compiler_params=pltpu.CompilerParams(vmem_limit_bytes=56 * 1024 * 1024),
    )(voltages, weights)


LEVELS = 4
TREE = 16
TAPS = 32
VMEM = 24 * 1024 * 1024


def taps_kernel(offsets_ref, shifts_ref, delays_ref, taps_ref):
    rows = lax.broadcasted_iota(jnp.int32, (LANES, LANES), 0)
    cols = lax.broadcasted_iota(jnp.int32, (LANES, LANES), 1)
    tree_row = rows & (TREE - 1)
    delay = jnp.broadcast_to(offsets_ref[...], (LANES, LANES)).astype(F32)
    for level in range(LEVELS):
        half = 2**level
        block = 2 * half
        here = (cols & (block - 1)) == (tree_row >> (LEVELS - 1 - level))
        held = jnp.where(here, shifts_ref[level : level + 1, :], 0).astype(F32).astype(BF16)
        reach = ((rows >> (level + 1)) == (cols >> (level + 1))) & ((cols & half) != 0)
        delay += jnp.dot(held, jnp.where(reach, 1.0, 0.0).astype(BF16), preferred_element_type=F32)
    groups = delays_ref.shape[1]
    row8 = lax.broadcasted_iota(jnp.int32, (groups, LANES), 0)
    col8 = lax.broadcasted_iota(jnp.int32, (groups, LANES), 1)
    of_group = jnp.where(row8 == (col8 >> LEVELS), 1.0, 0.0).astype(BF16)
    spread = jnp.dot(
        delays_ref[...].astype(F32).astype(BF16), of_group, preferred_element_type=F32
    )
    delay = delay.reshape(groups, TREE, LANES) + spread.reshape(groups, 1, LANES)
    delay = delay.reshape(LANES, LANES).astype(jnp.int32)
    for d in range(TAPS):
        taps_ref[:, d * LANES : (d + 1) * LANES] = jnp.where(delay == d, 1.0, 0.0).astype(BF16)


def make_taps(offsets, shifts, delays):
    return pl.pallas_call(
        taps_kernel,
        out_shape=pltpu.VMEM((LANES, TAPS * LANES), BF16),
        cost_estimate=pl.CostEstimate(flops=4_000_000, bytes_accessed=1_100_000, transcendentals=0),
    )(offsets.reshape(1, LANES), shifts, delays)


def normalize_kernel(binned_ref, baseline_ref, gains_ref, series_ref, head_ref):
    beams = baseline_ref.shape[1]
    per = LANES // TAPS
    baseline = baseline_ref[...]
    gains = gains_ref[...]
    heads = []
    for b in range(beams):
        x = binned_ref[pl.ds(b, LANES, stride=beams), :]
        x = ((x - baseline[:, b : b + 1]) * gains[:, b : b + 1]).astype(BF16)
        series_ref[b] = x
        heads.append(x.astype(F32)[:, :TAPS])
    for j in range(beams // per):
        head_ref[j] = jnp.concatenate(heads[j * per : (j + 1) * per], axis=1).astype(BF16)


def normalize(binned, baseline, gains):
    channels, beams = baseline.shape
    groups = beams * TAPS // LANES
    return pl.pallas_call(
        normalize_kernel,
        out_shape=(
            pltpu.VMEM((beams, channels, LANES), BF16),
            pltpu.VMEM((groups, channels, LANES), BF16),
        ),
        compiler_params=pltpu.CompilerParams(vmem_limit_bytes=VMEM),
        cost_estimate=pl.CostEstimate(flops=1_000_000, bytes_accessed=600_000, transcendentals=0),
    )(binned.reshape(channels * beams, LANES), baseline, gains)


def own_kernel(taps_ref, series_ref, out_ref, *windows):
    beams = series_ref.shape[0]
    lane = lax.broadcasted_iota(jnp.int32, (LANES, LANES), 1)
    for pair in range(beams // 2):
        window = windows[pair % len(windows)]
        for j in range(2):
            x = series_ref[2 * pair + j].astype(F32)
            for d in range(TAPS):
                moved = x if d == 0 else jnp.where(lane < LANES - d, pltpu.roll(x, LANES - d, 1), 0.0)
                window[d * LANES : (d + 1) * LANES, j * LANES : (j + 1) * LANES] = moved.astype(BF16)
        both = jnp.dot(taps_ref[...], window[...], preferred_element_type=F32)
        for j in range(2):
            out_ref[pl.ds(2 * pair + j, LANES, stride=beams), :] = both[:, j * LANES : (j + 1) * LANES]


def dedisperse_own(taps, series):
    beams = series.shape[0]
    return pl.pallas_call(
        own_kernel,
        out_shape=pltpu.VMEM((LANES * beams, LANES), F32),
        in_specs=[pl.BlockSpec(memory_space=pltpu.VMEM)] * 2,
        scratch_shapes=[pltpu.VMEM((TAPS * LANES, 2 * LANES), BF16)] * 2,
        compiler_params=pltpu.CompilerParams(vmem_limit_bytes=VMEM),
        cost_estimate=pl.CostEstimate(flops=4_000_000_000, bytes_accessed=3_000_000, transcendentals=0),
    )(taps, series)


def tail_kernel(taps_ref, tail_ref, own_ref, out_ref, window):
    groups = tail_ref.shape[0]
    per = LANES // TAPS
    beams = groups * per
    lane = lax.broadcasted_iota(jnp.int32, (LANES, LANES), 1)
    for j in range(groups):
        x = tail_ref[j].astype(F32)
        for d in range(TAPS):
            keep = (lane & (TAPS - 1)) >= TAPS - d
            moved = jnp.where(keep, pltpu.roll(x, (TAPS - d) % LANES, 1), 0.0)
            window[d * LANES : (d + 1) * LANES, j * LANES : (j + 1) * LANES] = moved.astype(BF16)
    added = jnp.dot(taps_ref[...], window[...], preferred_element_type=F32)
    last = lane >= LANES - TAPS
    for b in range(beams):
        rows = pl.ds(b, LANES, stride=beams)
        j, i = divmod(b, per)
        piece = added[:, j * LANES : (j + 1) * LANES]
        piece = pltpu.roll(piece, (per - 1 - i) * TAPS, 1)
        out_ref[rows, :] = own_ref[rows, :] + jnp.where(last, piece, 0.0)


def add_tail(taps, tail, own):
    return pl.pallas_call(
        tail_kernel,
        out_shape=jax.ShapeDtypeStruct(own.shape, F32),
        in_specs=[pl.BlockSpec(memory_space=pltpu.VMEM)] * 3,
        scratch_shapes=[pltpu.VMEM((TAPS * LANES, 2 * LANES), BF16)],
        compiler_params=pltpu.CompilerParams(vmem_limit_bytes=VMEM),
        cost_estimate=pl.CostEstimate(flops=1_000_000_000, bytes_accessed=2_000_000, transcendentals=0),
    )(taps, tail, own)


def from_behind(value, axis):
    count = lax.axis_size(axis)
    return lax.ppermute(value, axis, [(source, source - 1) for source in range(1, count)])


def per_device(voltages, weights, baseline, gains, offsets, shifts, delays):
    channels, beams = baseline.shape
    binned = beamform(voltages, weights)
    received = lax.all_to_all(binned, "chan", split_axis=0, concat_axis=0, tiled=True)
    taps = make_taps(offsets, shifts, delays)
    series, head = normalize(received, baseline, gains)
    following = from_behind(head, "tm")
    own = dedisperse_own(taps, series)
    return add_tail(taps, following, own).reshape(channels, beams, LANES)


def solution(mesh):
    placed = (
        P(None, "chan", None, "tm"),
        P(None, "chan", None, None),
        P(None, "chan"),
        P(None, "chan"),
        P(),
        P(),
        P(),
    )
    return jax.shard_map(
        per_device, mesh=mesh, in_specs=placed, out_specs=P(None, "chan", "tm"), check_vma=False
    )
```

```python
import functools
import jax
import jax.numpy as jnp
from jax import lax
from jax.experimental import pallas as pl
from jax.experimental.pallas import tpu as pltpu
from jax.sharding import PartitionSpec as P

LANES = 128
F32 = jnp.float32
BF16 = jnp.bfloat16
CENTRE = 32.0
SCALE = 2.0**-10


def fold_pair(a, b, stride):
    lane = lax.broadcasted_iota(jnp.int32, a.shape, 1)
    upper = (lane & stride) != 0
    return jnp.where(
        upper, b + pltpu.roll(b, stride, 1), a + pltpu.roll(a, LANES - stride, 1)
    )


def fold(tiles, stride):
    while len(tiles) > 1:
        tiles = [fold_pair(tiles[i], tiles[i + 1], stride) for i in range(0, len(tiles), 2)]
        stride *= 2
    return tiles[0]


def encode(binned):
    x = (binned - CENTRE) * SCALE
    square = x * x
    fourth = square * square
    eighth = fourth * fourth
    return jnp.where(x < 0.0, -eighth, eighth)


def decode(code):
    root = jnp.sqrt(jnp.sqrt(jnp.sqrt(jnp.abs(code)))) * (1.0 / SCALE)
    return jnp.where(code < 0.0, -root, root)


def beamform_kernel(chunk, width, late, v_hbm, w_hbm, out_ref, volts, weights, part, done, sem):
    channels, feeds, samples = v_hbm.shape[1:]
    beams = w_hbm.shape[2]
    steps = samples // width
    copies = {}
    count = 0
    for c in range(channels):
        copies[c, "w"] = pltpu.make_async_copy(w_hbm.at[:, c], weights.at[:, c], sem.at[count])
        count += 1
        if c == 0:
            for i, lanes in ((0, width), (1, samples - width)):
                here = pl.ds(i * width, lanes)
                copies[c, i] = pltpu.make_async_copy(v_hbm.at[:, c, :, here], volts.at[:, c, :, here], sem.at[count])
                count += 1
        else:
            copies[c, 0] = pltpu.make_async_copy(v_hbm.at[:, c], volts.at[:, c], sem.at[count])
            count += 1
    for copy in copies.values():
        copy.start()

    lane = lax.broadcasted_iota(jnp.int32, (chunk, LANES), 1)
    source = ((lane & 7) << 4) | (lane >> 3)

    def detect(c, i, r, both):
        real, imag = both[:chunk], both[chunk:]
        power = real * real + imag * imag
        piece = fold([power[:, k : k + LANES] for k in range(0, width, LANES)], 1)
        if i < steps - 1:
            part[i, r : r + chunk, :] = piece
            return
        tiles = [part[k, r : r + chunk, :] for k in range(steps - 1)] + [piece]
        total = jnp.take_along_axis(fold(tiles, width // LANES), source, axis=1)
        done[c, r : r + chunk, :] = encode(total)
        if c == channels - 1:
            blocks = [done[k, r : r + chunk, :].reshape(chunk // 8, 8, LANES) for k in range(channels)]
            out_ref[r // 8 : (r + chunk) // 8] = jnp.concatenate(blocks, axis=1).astype(BF16)

    waiting = []
    for c in range(channels):
        copies[c, "w"].wait()
        for i in range(steps):
            if (c, i) in copies:
                copies[c, i].wait()
            right = volts[:, c, :, i * width : (i + 1) * width].reshape(2 * feeds, width)
            for r in range(0, beams, chunk):
                w0, w1 = weights[0, c, r : r + chunk, :], weights[1, c, r : r + chunk, :]
                left = jnp.concatenate(
                    [jnp.concatenate([w0, -w1], axis=1), jnp.concatenate([w1, w0], axis=1)], axis=0
                )
                both = jnp.dot(left, right, preferred_element_type=F32)
                waiting.append((c, i, r, both))
                if len(waiting) > late:
                    detect(*waiting.pop(0))
    for item in waiting:
        detect(*item)


def beamform(voltages, weights, chunk=256, width=512, late=1):
    _, channels, feeds, samples = voltages.shape
    beams = weights.shape[2]
    return pl.pallas_call(
        functools.partial(beamform_kernel, chunk, width, late),
        in_specs=[pl.BlockSpec(memory_space=pl.ANY)] * 2,
        out_shape=jax.ShapeDtypeStruct((beams // 8, 8 * channels, LANES), BF16),
        scratch_shapes=[
            pltpu.VMEM(voltages.shape, BF16),
            pltpu.VMEM(weights.shape, BF16),
            pltpu.VMEM((samples // width - 1, beams, LANES), F32),
            pltpu.VMEM((channels, beams, LANES), F32),
            pltpu.SemaphoreType.DMA((16,)),
        ],
        compiler_params=pltpu.CompilerParams(vmem_limit_bytes=56 * 1024 * 1024),
    )(voltages, weights)


LEVELS = 4
TREE = 16
TAPS = 32
VMEM = 24 * 1024 * 1024


def taps_kernel(offsets_ref, shifts_ref, delays_ref, taps_ref):
    rows = lax.broadcasted_iota(jnp.int32, (LANES, LANES), 0)
    cols = lax.broadcasted_iota(jnp.int32, (LANES, LANES), 1)
    tree_row = rows & (TREE - 1)
    delay = jnp.broadcast_to(offsets_ref[...], (LANES, LANES)).astype(F32)
    for level in range(LEVELS):
        half = 2**level
        block = 2 * half
        here = (cols & (block - 1)) == (tree_row >> (LEVELS - 1 - level))
        held = jnp.where(here, shifts_ref[level : level + 1, :], 0).astype(F32).astype(BF16)
        reach = ((rows >> (level + 1)) == (cols >> (level + 1))) & ((cols & half) != 0)
        delay += jnp.dot(held, jnp.where(reach, 1.0, 0.0).astype(BF16), preferred_element_type=F32)
    groups = delays_ref.shape[1]
    row8 = lax.broadcasted_iota(jnp.int32, (groups, LANES), 0)
    col8 = lax.broadcasted_iota(jnp.int32, (groups, LANES), 1)
    of_group = jnp.where(row8 == (col8 >> LEVELS), 1.0, 0.0).astype(BF16)
    spread = jnp.dot(
        delays_ref[...].astype(F32).astype(BF16), of_group, preferred_element_type=F32
    )
    delay = delay.reshape(groups, TREE, LANES) + spread.reshape(groups, 1, LANES)
    delay = delay.reshape(LANES, LANES).astype(jnp.int32)
    for d in range(TAPS):
        taps_ref[:, d * LANES : (d + 1) * LANES] = jnp.where(delay == d, 1.0, 0.0).astype(BF16)


def make_taps(offsets, shifts, delays):
    return pl.pallas_call(
        taps_kernel,
        out_shape=pltpu.VMEM((LANES, TAPS * LANES), BF16),
        cost_estimate=pl.CostEstimate(flops=4_000_000, bytes_accessed=1_100_000, transcendentals=0),
    )(offsets.reshape(1, LANES), shifts, delays)


def normalize_kernel(received_ref, baseline_ref, gains_ref, series_ref, head_ref, wide):
    beams = baseline_ref.shape[1]
    per = LANES // TAPS
    wide[...] = decode(received_ref[...].astype(F32)).reshape(wide.shape)
    above = baseline_ref[...] - CENTRE
    gains = gains_ref[...]
    heads = []
    for b in range(beams):
        x = wide[pl.ds(b, LANES, stride=beams), :]
        x = ((x - above[:, b : b + 1]) * gains[:, b : b + 1]).astype(BF16)
        series_ref[b] = x
        heads.append(x.astype(F32)[:, :TAPS])
    for j in range(beams // per):
        head_ref[j] = jnp.concatenate(heads[j * per : (j + 1) * per], axis=1).astype(BF16)


def normalize(received, baseline, gains):
    channels, beams = baseline.shape
    groups = beams * TAPS // LANES
    return pl.pallas_call(
        normalize_kernel,
        out_shape=(
            pltpu.VMEM((beams, channels, LANES), BF16),
            pltpu.VMEM((groups, channels, LANES), BF16),
        ),
        scratch_shapes=[pltpu.VMEM((channels * beams, LANES), F32)],
        compiler_params=pltpu.CompilerParams(vmem_limit_bytes=VMEM),
        cost_estimate=pl.CostEstimate(flops=1_000_000, bytes_accessed=600_000, transcendentals=0),
    )(received, baseline, gains)


def own_kernel(taps_ref, series_ref, out_ref, *windows):
    beams = series_ref.shape[0]
    lane = lax.broadcasted_iota(jnp.int32, (LANES, LANES), 1)
    for pair in range(beams // 2):
        window = windows[pair % len(windows)]
        for j in range(2):
            x = series_ref[2 * pair + j].astype(F32)
            for d in range(TAPS):
                moved = x if d == 0 else jnp.where(lane < LANES - d, pltpu.roll(x, LANES - d, 1), 0.0)
                window[d * LANES : (d + 1) * LANES, j * LANES : (j + 1) * LANES] = moved.astype(BF16)
        both = jnp.dot(taps_ref[...], window[...], preferred_element_type=F32)
        for j in range(2):
            out_ref[pl.ds(2 * pair + j, LANES, stride=beams), :] = both[:, j * LANES : (j + 1) * LANES]


def dedisperse_own(taps, series):
    beams = series.shape[0]
    return pl.pallas_call(
        own_kernel,
        out_shape=pltpu.VMEM((LANES * beams, LANES), F32),
        in_specs=[pl.BlockSpec(memory_space=pltpu.VMEM)] * 2,
        scratch_shapes=[pltpu.VMEM((TAPS * LANES, 2 * LANES), BF16)] * 2,
        compiler_params=pltpu.CompilerParams(vmem_limit_bytes=VMEM),
        cost_estimate=pl.CostEstimate(flops=4_000_000_000, bytes_accessed=3_000_000, transcendentals=0),
    )(taps, series)


def tail_kernel(taps_ref, tail_ref, own_ref, out_ref, window):
    groups = tail_ref.shape[0]
    per = LANES // TAPS
    beams = groups * per
    lane = lax.broadcasted_iota(jnp.int32, (LANES, LANES), 1)
    for j in range(groups):
        x = tail_ref[j].astype(F32)
        for d in range(TAPS):
            keep = (lane & (TAPS - 1)) >= TAPS - d
            moved = jnp.where(keep, pltpu.roll(x, (TAPS - d) % LANES, 1), 0.0)
            window[d * LANES : (d + 1) * LANES, j * LANES : (j + 1) * LANES] = moved.astype(BF16)
    added = jnp.dot(taps_ref[...], window[...], preferred_element_type=F32)
    last = lane >= LANES - TAPS
    for b in range(beams):
        rows = pl.ds(b, LANES, stride=beams)
        j, i = divmod(b, per)
        piece = added[:, j * LANES : (j + 1) * LANES]
        piece = pltpu.roll(piece, (per - 1 - i) * TAPS, 1)
        out_ref[rows, :] = own_ref[rows, :] + jnp.where(last, piece, 0.0)


def add_tail(taps, tail, own):
    return pl.pallas_call(
        tail_kernel,
        out_shape=jax.ShapeDtypeStruct(own.shape, F32),
        in_specs=[pl.BlockSpec(memory_space=pltpu.VMEM)] * 3,
        scratch_shapes=[pltpu.VMEM((TAPS * LANES, 2 * LANES), BF16)],
        compiler_params=pltpu.CompilerParams(vmem_limit_bytes=VMEM),
        cost_estimate=pl.CostEstimate(flops=1_000_000_000, bytes_accessed=2_000_000, transcendentals=0),
    )(taps, tail, own)


def from_behind(value, axis):
    count = lax.axis_size(axis)
    return lax.ppermute(value, axis, [(source, source - 1) for source in range(1, count)])


def per_device(voltages, weights, baseline, gains, offsets, shifts, delays):
    channels, beams = baseline.shape
    codes = beamform(voltages, weights)
    received = lax.all_to_all(codes, "chan", split_axis=0, concat_axis=0, tiled=True)
    taps = make_taps(offsets, shifts, delays)
    series, head = normalize(received, baseline, gains)
    following = from_behind(head, "tm")
    own = dedisperse_own(taps, series)
    return add_tail(taps, following, own).reshape(channels, beams, LANES)


def solution(mesh):
    placed = (
        P(None, "chan", None, "tm"),
        P(None, "chan", None, None),
        P(None, "chan"),
        P(None, "chan"),
        P(),
        P(),
        P(),
    )
    return jax.shard_map(
        per_device, mesh=mesh, in_specs=placed, out_specs=P(None, "chan", "tm"), check_vma=False
    )
```

```python
import functools
import jax
import jax.numpy as jnp
from jax import lax
from jax.experimental import pallas as pl
from jax.experimental.pallas import tpu as pltpu
from jax.sharding import PartitionSpec as P

LANES = 128
F32 = jnp.float32
BF16 = jnp.bfloat16
CENTRE = 32.0
SCALE = 2.0**-10


def fold_pair(a, b, stride):
    lane = lax.broadcasted_iota(jnp.int32, a.shape, 1)
    upper = (lane & stride) != 0
    return jnp.where(
        upper, b + pltpu.roll(b, stride, 1), a + pltpu.roll(a, LANES - stride, 1)
    )


def fold(tiles, stride):
    while len(tiles) > 1:
        tiles = [fold_pair(tiles[i], tiles[i + 1], stride) for i in range(0, len(tiles), 2)]
        stride *= 2
    return tiles[0]


def encode(binned):
    x = (binned - CENTRE) * SCALE
    square = x * x
    fourth = square * square
    eighth = fourth * fourth
    return jnp.where(x < 0.0, -eighth, eighth)


def decode(code):
    root = jnp.exp2(jnp.log2(jnp.abs(code)) * 0.125) * (1.0 / SCALE)
    return jnp.where(code < 0.0, -root, root)


def beamform_kernel(chunk, width, late, v_hbm, w_hbm, out_ref, volts, weights, part, done, sem):
    channels, feeds, samples = v_hbm.shape[1:]
    beams = w_hbm.shape[2]
    steps = samples // width
    copies = {}
    count = 0
    for c in range(channels):
        copies[c, "w"] = pltpu.make_async_copy(w_hbm.at[:, c], weights.at[:, c], sem.at[count])
        count += 1
        if c == 0:
            for i, lanes in ((0, width), (1, samples - width)):
                here = pl.ds(i * width, lanes)
                copies[c, i] = pltpu.make_async_copy(v_hbm.at[:, c, :, here], volts.at[:, c, :, here], sem.at[count])
                count += 1
        else:
            copies[c, 0] = pltpu.make_async_copy(v_hbm.at[:, c], volts.at[:, c], sem.at[count])
            count += 1
    for copy in copies.values():
        copy.start()

    lane = lax.broadcasted_iota(jnp.int32, (chunk, LANES), 1)
    source = ((lane & 7) << 4) | (lane >> 3)

    def detect(c, i, r, both):
        real, imag = both[:chunk], both[chunk:]
        power = real * real + imag * imag
        piece = fold([power[:, k : k + LANES] for k in range(0, width, LANES)], 1)
        if i < steps - 1:
            part[i, r : r + chunk, :] = piece
            return
        tiles = [part[k, r : r + chunk, :] for k in range(steps - 1)] + [piece]
        total = jnp.take_along_axis(fold(tiles, width // LANES), source, axis=1)
        done[c, r : r + chunk, :] = encode(total)
        if c == channels - 1:
            blocks = [done[k, r : r + chunk, :].reshape(chunk // 8, 8, LANES) for k in range(channels)]
            out_ref[r // 8 : (r + chunk) // 8] = jnp.concatenate(blocks, axis=1).astype(BF16)

    waiting = []
    for c in range(channels):
        copies[c, "w"].wait()
        for i in range(steps):
            if (c, i) in copies:
                copies[c, i].wait()
            right = volts[:, c, :, i * width : (i + 1) * width].reshape(2 * feeds, width)
            for r in range(0, beams, chunk):
                w0, w1 = weights[0, c, r : r + chunk, :], weights[1, c, r : r + chunk, :]
                left = jnp.concatenate(
                    [jnp.concatenate([w0, -w1], axis=1), jnp.concatenate([w1, w0], axis=1)], axis=0
                )
                both = jnp.dot(left, right, preferred_element_type=F32)
                waiting.append((c, i, r, both))
                if len(waiting) > late:
                    detect(*waiting.pop(0))
    for item in waiting:
        detect(*item)


def beamform(voltages, weights, chunk=256, width=512, late=1):
    _, channels, feeds, samples = voltages.shape
    beams = weights.shape[2]
    return pl.pallas_call(
        functools.partial(beamform_kernel, chunk, width, late),
        in_specs=[pl.BlockSpec(memory_space=pl.ANY)] * 2,
        out_shape=jax.ShapeDtypeStruct((beams // 8, 8 * channels, LANES), BF16),
        scratch_shapes=[
            pltpu.VMEM(voltages.shape, BF16),
            pltpu.VMEM(weights.shape, BF16),
            pltpu.VMEM((samples // width - 1, beams, LANES), F32),
            pltpu.VMEM((channels, beams, LANES), F32),
            pltpu.SemaphoreType.DMA((16,)),
        ],
        compiler_params=pltpu.CompilerParams(vmem_limit_bytes=56 * 1024 * 1024),
    )(voltages, weights)


LEVELS = 4
TREE = 16
TAPS = 32
VMEM = 24 * 1024 * 1024


def taps_kernel(offsets_ref, shifts_ref, delays_ref, taps_ref):
    rows = lax.broadcasted_iota(jnp.int32, (LANES, LANES), 0)
    cols = lax.broadcasted_iota(jnp.int32, (LANES, LANES), 1)
    tree_row = rows & (TREE - 1)
    delay = jnp.broadcast_to(offsets_ref[...], (LANES, LANES)).astype(F32)
    for level in range(LEVELS):
        half = 2**level
        block = 2 * half
        here = (cols & (block - 1)) == (tree_row >> (LEVELS - 1 - level))
        held = jnp.where(here, shifts_ref[level : level + 1, :], 0).astype(F32).astype(BF16)
        reach = ((rows >> (level + 1)) == (cols >> (level + 1))) & ((cols & half) != 0)
        delay += jnp.dot(held, jnp.where(reach, 1.0, 0.0).astype(BF16), preferred_element_type=F32)
    groups = delays_ref.shape[1]
    row8 = lax.broadcasted_iota(jnp.int32, (groups, LANES), 0)
    col8 = lax.broadcasted_iota(jnp.int32, (groups, LANES), 1)
    of_group = jnp.where(row8 == (col8 >> LEVELS), 1.0, 0.0).astype(BF16)
    spread = jnp.dot(
        delays_ref[...].astype(F32).astype(BF16), of_group, preferred_element_type=F32
    )
    delay = delay.reshape(groups, TREE, LANES) + spread.reshape(groups, 1, LANES)
    delay = delay.reshape(LANES, LANES).astype(jnp.int32)
    for d in range(TAPS):
        taps_ref[:, d * LANES : (d + 1) * LANES] = jnp.where(delay == d, 1.0, 0.0).astype(BF16)


def make_taps(offsets, shifts, delays):
    return pl.pallas_call(
        taps_kernel,
        out_shape=pltpu.VMEM((LANES, TAPS * LANES), BF16),
        cost_estimate=pl.CostEstimate(flops=4_000_000, bytes_accessed=1_100_000, transcendentals=0),
    )(offsets.reshape(1, LANES), shifts, delays)


def head_kernel(codes_ref, baseline_ref, gains_ref, head_ref, wide):
    beams = baseline_ref.shape[1]
    per = LANES // TAPS
    wide[...] = codes_ref[...].astype(F32).reshape(wide.shape)
    above = baseline_ref[...] - CENTRE
    gains = gains_ref[...]
    lane = lax.broadcasted_iota(jnp.int32, (LANES, LANES), 1)
    for j in range(beams // per):
        packed, floor, gain = None, None, None
        for i in range(per):
            b = j * per + i
            x = wide[pl.ds(b, LANES, stride=beams), :]
            x = x if i == 0 else pltpu.roll(x, i * TAPS, 1)
            low = jnp.broadcast_to(above[:, b : b + 1], x.shape)
            up = jnp.broadcast_to(gains[:, b : b + 1], x.shape)
            if i == 0:
                packed, floor, gain = x, low, up
            else:
                here = lane >= i * TAPS
                packed = jnp.where(here, x, packed)
                floor = jnp.where(here, low, floor)
                gain = jnp.where(here, up, gain)
        head_ref[j] = ((decode(packed) - floor) * gain).astype(BF16)


def make_head(codes, baseline, gains):
    channels, beams = baseline.shape
    return pl.pallas_call(
        head_kernel,
        out_shape=pltpu.VMEM((beams * TAPS // LANES, channels, LANES), BF16),
        scratch_shapes=[pltpu.VMEM((channels * beams, LANES), F32)],
        compiler_params=pltpu.CompilerParams(vmem_limit_bytes=VMEM),
        cost_estimate=pl.CostEstimate(flops=1_000_000, bytes_accessed=400_000, transcendentals=0),
    )(codes, baseline, gains)


def own_kernel(taps_ref, codes_ref, baseline_ref, gains_ref, out_ref, wide, *windows):
    beams = baseline_ref.shape[1]
    wide[...] = codes_ref[...].astype(F32).reshape(wide.shape)
    above = baseline_ref[...] - CENTRE
    gains = gains_ref[...]
    lane = lax.broadcasted_iota(jnp.int32, (LANES, LANES), 1)
    for pair in range(beams // 2):
        window = windows[pair % len(windows)]
        for j in range(2):
            b = 2 * pair + j
            x = decode(wide[pl.ds(b, LANES, stride=beams), :])
            x = ((x - above[:, b : b + 1]) * gains[:, b : b + 1]).astype(BF16)
            x = x.astype(F32)
            for d in range(TAPS):
                moved = x if d == 0 else jnp.where(lane < LANES - d, pltpu.roll(x, LANES - d, 1), 0.0)
                window[d * LANES : (d + 1) * LANES, j * LANES : (j + 1) * LANES] = moved.astype(BF16)
        both = jnp.dot(taps_ref[...], window[...], preferred_element_type=F32)
        for j in range(2):
            out_ref[pl.ds(2 * pair + j, LANES, stride=beams), :] = both[:, j * LANES : (j + 1) * LANES]


def dedisperse_own(taps, codes, baseline, gains):
    channels, beams = baseline.shape
    return pl.pallas_call(
        own_kernel,
        out_shape=pltpu.VMEM((LANES * beams, LANES), F32),
        in_specs=[pl.BlockSpec(memory_space=pltpu.VMEM)] * 4,
        scratch_shapes=[pltpu.VMEM((channels * beams, LANES), F32)]
        + [pltpu.VMEM((TAPS * LANES, 2 * LANES), BF16)] * 2,
        compiler_params=pltpu.CompilerParams(vmem_limit_bytes=VMEM),
        cost_estimate=pl.CostEstimate(flops=4_000_000_000, bytes_accessed=3_000_000, transcendentals=0),
    )(taps, codes, baseline, gains)


def tail_kernel(taps_ref, tail_ref, own_ref, out_hbm, window, total, sem):
    groups = tail_ref.shape[0]
    per = LANES // TAPS
    beams = groups * per
    lane = lax.broadcasted_iota(jnp.int32, (LANES, LANES), 1)
    for j in range(groups):
        x = tail_ref[j].astype(F32)
        for d in range(TAPS):
            keep = (lane & (TAPS - 1)) >= TAPS - d
            moved = jnp.where(keep, pltpu.roll(x, (TAPS - d) % LANES, 1), 0.0)
            window[d * LANES : (d + 1) * LANES, j * LANES : (j + 1) * LANES] = moved.astype(BF16)
    added = jnp.dot(taps_ref[...], window[...], preferred_element_type=F32)
    last = lax.broadcasted_iota(jnp.int32, (TREE, LANES), 1) >= LANES - TAPS
    copies = []
    for q in range(LANES // TREE):
        for b in range(beams):
            rows = pl.ds(q * TREE * beams + b, TREE, stride=beams)
            j, i = divmod(b, per)
            piece = added[q * TREE : (q + 1) * TREE, j * LANES : (j + 1) * LANES]
            piece = pltpu.roll(piece, (per - 1 - i) * TAPS, 1)
            total[rows, :] = own_ref[rows, :] + jnp.where(last, piece, 0.0)
        block = pl.ds(q * TREE * beams, TREE * beams)
        copies.append(pltpu.make_async_copy(total.at[block], out_hbm.at[block], sem.at[q]))
        copies[-1].start()
    for copy in copies:
        copy.wait()


def add_tail(taps, tail, own):
    return pl.pallas_call(
        tail_kernel,
        out_shape=jax.ShapeDtypeStruct(own.shape, F32),
        in_specs=[pl.BlockSpec(memory_space=pltpu.VMEM)] * 3,
        out_specs=pl.BlockSpec(memory_space=pl.ANY),
        scratch_shapes=[
            pltpu.VMEM((TAPS * LANES, 2 * LANES), BF16),
            pltpu.VMEM(own.shape, F32),
            pltpu.SemaphoreType.DMA((LANES // TREE,)),
        ],
        compiler_params=pltpu.CompilerParams(vmem_limit_bytes=VMEM),
        cost_estimate=pl.CostEstimate(flops=1_000_000_000, bytes_accessed=2_000_000, transcendentals=0),
    )(taps, tail, own)


def from_behind(value, axis):
    count = lax.axis_size(axis)
    return lax.ppermute(value, axis, [(source, source - 1) for source in range(1, count)])


def per_device(voltages, weights, baseline, gains, offsets, shifts, delays):
    channels, beams = baseline.shape
    codes = beamform(voltages, weights)
    received = lax.all_to_all(codes, "chan", split_axis=0, concat_axis=0, tiled=True)
    taps = make_taps(offsets, shifts, delays)
    following = from_behind(make_head(received, baseline, gains), "tm")
    own = dedisperse_own(taps, received, baseline, gains)
    return add_tail(taps, following, own).reshape(channels, beams, LANES)


def solution(mesh):
    placed = (
        P(None, "chan", None, "tm"),
        P(None, "chan", None, None),
        P(None, "chan"),
        P(None, "chan"),
        P(),
        P(),
        P(),
    )
    return jax.shard_map(
        per_device, mesh=mesh, in_specs=placed, out_specs=P(None, "chan", "tm"), check_vma=False
    )
```

```python
import functools
import jax
import jax.numpy as jnp
from jax import lax
from jax.experimental import pallas as pl
from jax.experimental.pallas import tpu as pltpu
from jax.sharding import PartitionSpec as P

LANES = 128
F32 = jnp.float32
BF16 = jnp.bfloat16
CENTRE = 32.0
SCALE = 2.0**-10


def fold_pair(a, b, stride):
    lane = lax.broadcasted_iota(jnp.int32, a.shape, 1)
    upper = (lane & stride) != 0
    return jnp.where(
        upper, b + pltpu.roll(b, stride, 1), a + pltpu.roll(a, LANES - stride, 1)
    )


def fold(tiles, stride):
    while len(tiles) > 1:
        tiles = [fold_pair(tiles[i], tiles[i + 1], stride) for i in range(0, len(tiles), 2)]
        stride *= 2
    return tiles[0]


def encode(binned):
    x = (binned - CENTRE) * SCALE
    square = x * x
    fourth = square * square
    eighth = fourth * fourth
    return jnp.where(x < 0.0, -eighth, eighth)


def decode(code):
    root = jnp.exp2(jnp.log2(jnp.abs(code)) * 0.125) * (1.0 / SCALE)
    return jnp.where(code < 0.0, -root, root)


def beamform_kernel(chunk, width, late, v_hbm, w_hbm, out_ref, volts, weights, part, done, sem):
    channels, feeds, samples = v_hbm.shape[1:]
    beams = w_hbm.shape[2]
    steps = samples // width
    copies = {}
    count = 0
    for c in range(channels):
        copies[c, "w"] = pltpu.make_async_copy(w_hbm.at[:, c], weights.at[:, c], sem.at[count])
        count += 1
        if c == 0:
            for i, lanes in ((0, width), (1, samples - width)):
                here = pl.ds(i * width, lanes)
                copies[c, i] = pltpu.make_async_copy(v_hbm.at[:, c, :, here], volts.at[:, c, :, here], sem.at[count])
                count += 1
        else:
            copies[c, 0] = pltpu.make_async_copy(v_hbm.at[:, c], volts.at[:, c], sem.at[count])
            count += 1
    for copy in copies.values():
        copy.start()

    lane = lax.broadcasted_iota(jnp.int32, (chunk, LANES), 1)
    source = ((lane & 7) << 4) | (lane >> 3)

    def detect(c, i, r, both):
        real, imag = both[:chunk], both[chunk:]
        power = real * real + imag * imag
        piece = fold([power[:, k : k + LANES] for k in range(0, width, LANES)], 1)
        if i < steps - 1:
            part[i, r : r + chunk, :] = piece
            return
        tiles = [part[k, r : r + chunk, :] for k in range(steps - 1)] + [piece]
        total = jnp.take_along_axis(fold(tiles, width // LANES), source, axis=1)
        done[c, r : r + chunk, :] = encode(total)
        if c == channels - 1:
            blocks = [done[k, r : r + chunk, :].reshape(chunk // 8, 8, LANES) for k in range(channels)]
            out_ref[r // 8 : (r + chunk) // 8] = jnp.concatenate(blocks, axis=1).astype(BF16)

    waiting = []
    for c in range(channels):
        copies[c, "w"].wait()
        for i in range(steps):
            if (c, i) in copies:
                copies[c, i].wait()
            right = volts[:, c, :, i * width : (i + 1) * width].reshape(2 * feeds, width)
            for r in range(0, beams, chunk):
                w0, w1 = weights[0, c, r : r + chunk, :], weights[1, c, r : r + chunk, :]
                left = jnp.concatenate(
                    [jnp.concatenate([w0, -w1], axis=1), jnp.concatenate([w1, w0], axis=1)], axis=0
                )
                both = jnp.dot(left, right, preferred_element_type=F32)
                waiting.append((c, i, r, both))
                if len(waiting) > late:
                    detect(*waiting.pop(0))
    for item in waiting:
        detect(*item)


def beamform(voltages, weights, chunk=256, width=512, late=1):
    _, channels, feeds, samples = voltages.shape
    beams = weights.shape[2]
    return pl.pallas_call(
        functools.partial(beamform_kernel, chunk, width, late),
        in_specs=[pl.BlockSpec(memory_space=pl.ANY)] * 2,
        out_shape=jax.ShapeDtypeStruct((beams // 8, 8 * channels, LANES), BF16),
        scratch_shapes=[
            pltpu.VMEM(voltages.shape, BF16),
            pltpu.VMEM(weights.shape, BF16),
            pltpu.VMEM((samples // width - 1, beams, LANES), F32),
            pltpu.VMEM((channels, beams, LANES), F32),
            pltpu.SemaphoreType.DMA((16,)),
        ],
        compiler_params=pltpu.CompilerParams(vmem_limit_bytes=56 * 1024 * 1024),
    )(voltages, weights)


LEVELS = 4
TREE = 16
TAPS = 32
FINE = 8
VMEM = 24 * 1024 * 1024


def taps_kernel(offsets_ref, shifts_ref, delays_ref, taps_ref):
    rows = lax.broadcasted_iota(jnp.int32, (LANES, LANES), 0)
    cols = lax.broadcasted_iota(jnp.int32, (LANES, LANES), 1)
    tree_row = rows & (TREE - 1)
    delay = jnp.broadcast_to(offsets_ref[...], (LANES, LANES)).astype(F32)
    for level in range(LEVELS):
        half = 2**level
        block = 2 * half
        here = (cols & (block - 1)) == (tree_row >> (LEVELS - 1 - level))
        held = jnp.where(here, shifts_ref[level : level + 1, :], 0).astype(F32).astype(BF16)
        reach = ((rows >> (level + 1)) == (cols >> (level + 1))) & ((cols & half) != 0)
        delay += jnp.dot(held, jnp.where(reach, 1.0, 0.0).astype(BF16), preferred_element_type=F32)
    groups = delays_ref.shape[1]
    row8 = lax.broadcasted_iota(jnp.int32, (groups, LANES), 0)
    col8 = lax.broadcasted_iota(jnp.int32, (groups, LANES), 1)
    of_group = jnp.where(row8 == (col8 >> LEVELS), 1.0, 0.0).astype(BF16)
    spread = jnp.dot(
        delays_ref[...].astype(F32).astype(BF16), of_group, preferred_element_type=F32
    )
    delay = delay.reshape(groups, TREE, LANES) + spread.reshape(groups, 1, LANES)
    delay = delay.reshape(LANES, LANES).astype(jnp.int32)
    for d in range(TAPS):
        taps_ref[:, d * LANES : (d + 1) * LANES] = jnp.where(delay == d, 1.0, 0.0).astype(BF16)


def make_taps(offsets, shifts, delays):
    return pl.pallas_call(
        taps_kernel,
        out_shape=pltpu.VMEM((LANES, TAPS * LANES), BF16),
        cost_estimate=pl.CostEstimate(flops=4_000_000, bytes_accessed=1_100_000, transcendentals=0),
    )(offsets.reshape(1, LANES), shifts, delays)


def head_kernel(codes_ref, baseline_ref, gains_ref, head_ref, wide):
    beams = baseline_ref.shape[1]
    per = LANES // TAPS
    wide[...] = codes_ref[...].astype(F32).reshape(wide.shape)
    above = baseline_ref[...] - CENTRE
    gains = gains_ref[...]
    lane = lax.broadcasted_iota(jnp.int32, (LANES, LANES), 1)
    for j in range(beams // per):
        packed, floor, gain = None, None, None
        for i in range(per):
            b = j * per + i
            x = wide[pl.ds(b, LANES, stride=beams), :]
            x = x if i == 0 else pltpu.roll(x, i * TAPS, 1)
            low = jnp.broadcast_to(above[:, b : b + 1], x.shape)
            up = jnp.broadcast_to(gains[:, b : b + 1], x.shape)
            if i == 0:
                packed, floor, gain = x, low, up
            else:
                here = lane >= i * TAPS
                packed = jnp.where(here, x, packed)
                floor = jnp.where(here, low, floor)
                gain = jnp.where(here, up, gain)
        head_ref[j] = ((decode(packed) - floor) * gain).astype(BF16)


def make_head(codes, baseline, gains):
    channels, beams = baseline.shape
    return pl.pallas_call(
        head_kernel,
        out_shape=pltpu.VMEM((beams * TAPS // LANES, channels, LANES), BF16),
        scratch_shapes=[pltpu.VMEM((channels * beams, LANES), F32)],
        compiler_params=pltpu.CompilerParams(vmem_limit_bytes=VMEM),
        cost_estimate=pl.CostEstimate(flops=1_000_000, bytes_accessed=400_000, transcendentals=0),
    )(codes, baseline, gains)


def own_kernel(taps_ref, codes_ref, baseline_ref, gains_ref, out_ref, wide, *windows):
    beams = baseline_ref.shape[1]
    wide[...] = codes_ref[...].astype(F32).reshape(wide.shape)
    above = baseline_ref[...] - CENTRE
    gains = gains_ref[...]
    lane = lax.broadcasted_iota(jnp.int32, (LANES, LANES), 1)
    for pair in range(beams // 2):
        window = windows[pair % len(windows)]
        for j in range(2):
            b = 2 * pair + j
            x = decode(wide[pl.ds(b, LANES, stride=beams), :])
            x = ((x - above[:, b : b + 1]) * gains[:, b : b + 1]).astype(BF16)
            x = x.astype(F32)
            for d in range(TAPS):
                moved = x if d == 0 else jnp.where(lane < LANES - d, pltpu.roll(x, LANES - d, 1), 0.0)
                window[d * LANES : (d + 1) * LANES, j * LANES : (j + 1) * LANES] = moved.astype(BF16)
        both = jnp.dot(taps_ref[...], window[...], preferred_element_type=F32)
        for j in range(2):
            out_ref[pl.ds(2 * pair + j, LANES, stride=beams), :] = both[:, j * LANES : (j + 1) * LANES]


def dedisperse_own(taps, codes, baseline, gains):
    channels, beams = baseline.shape
    return pl.pallas_call(
        own_kernel,
        out_shape=pltpu.VMEM((LANES * beams, LANES), F32),
        in_specs=[pl.BlockSpec(memory_space=pltpu.VMEM)] * 4,
        scratch_shapes=[pltpu.VMEM((channels * beams, LANES), F32)]
        + [pltpu.VMEM((TAPS * LANES, 2 * LANES), BF16)] * 2,
        compiler_params=pltpu.CompilerParams(vmem_limit_bytes=VMEM),
        cost_estimate=pl.CostEstimate(flops=4_000_000_000, bytes_accessed=3_000_000, transcendentals=0),
    )(taps, codes, baseline, gains)


def tail_kernel(taps_ref, tail_ref, own_ref, out_hbm, window, total, sem):
    groups = tail_ref.shape[0]
    per = LANES // TAPS
    beams = groups * per
    lane = lax.broadcasted_iota(jnp.int32, (LANES, LANES), 1) & (TAPS - 1)
    for j in range(groups):
        x = tail_ref[j].astype(F32)
        for e in range(FINE):
            moved = jnp.where(lane >= FINE - e, pltpu.roll(x, FINE - e, 1), 0.0)
            window[e * LANES : (e + 1) * LANES, j * LANES : (j + 1) * LANES] = moved.astype(BF16)
    depth = FINE * LANES
    coarse = jnp.concatenate([taps_ref[:, a * depth : (a + 1) * depth] for a in range(TAPS // FINE)], axis=0)
    sums = jnp.dot(coarse, window[...], preferred_element_type=F32)
    added = []
    for j in range(groups):
        whole = None
        for a in range(TAPS // FINE):
            y = sums[a * LANES : (a + 1) * LANES, j * LANES : (j + 1) * LANES]
            steps = TAPS - FINE - a * FINE
            if steps:
                y = jnp.where(lane >= steps, pltpu.roll(y, steps, 1), 0.0)
            whole = y if whole is None else whole + y
        added.append(whole)
    last = lax.broadcasted_iota(jnp.int32, (TREE, LANES), 1) >= LANES - TAPS
    copies = []
    for q in range(LANES // TREE):
        for b in range(beams):
            rows = pl.ds(q * TREE * beams + b, TREE, stride=beams)
            j, i = divmod(b, per)
            piece = added[j][q * TREE : (q + 1) * TREE, :]
            piece = pltpu.roll(piece, (per - 1 - i) * TAPS, 1)
            total[rows, :] = own_ref[rows, :] + jnp.where(last, piece, 0.0)
        block = pl.ds(q * TREE * beams, TREE * beams)
        copies.append(pltpu.make_async_copy(total.at[block], out_hbm.at[block], sem.at[q]))
        copies[-1].start()
    for copy in copies:
        copy.wait()


def add_tail(taps, tail, own):
    return pl.pallas_call(
        tail_kernel,
        out_shape=jax.ShapeDtypeStruct(own.shape, F32),
        in_specs=[pl.BlockSpec(memory_space=pltpu.VMEM)] * 3,
        out_specs=pl.BlockSpec(memory_space=pl.ANY),
        scratch_shapes=[
            pltpu.VMEM((FINE * LANES, 2 * LANES), BF16),
            pltpu.VMEM(own.shape, F32),
            pltpu.SemaphoreType.DMA((LANES // TREE,)),
        ],
        compiler_params=pltpu.CompilerParams(vmem_limit_bytes=VMEM),
        cost_estimate=pl.CostEstimate(flops=1_000_000_000, bytes_accessed=2_000_000, transcendentals=0),
    )(taps, tail, own)


def from_behind(value, axis):
    count = lax.axis_size(axis)
    return lax.ppermute(value, axis, [(source, source - 1) for source in range(1, count)])


def per_device(voltages, weights, baseline, gains, offsets, shifts, delays):
    channels, beams = baseline.shape
    codes = beamform(voltages, weights)
    received = lax.all_to_all(codes, "chan", split_axis=0, concat_axis=0, tiled=True)
    taps = make_taps(offsets, shifts, delays)
    following = from_behind(make_head(received, baseline, gains), "tm")
    own = dedisperse_own(taps, received, baseline, gains)
    return add_tail(taps, following, own).reshape(channels, beams, LANES)


def solution(mesh):
    placed = (
        P(None, "chan", None, "tm"),
        P(None, "chan", None, None),
        P(None, "chan"),
        P(None, "chan"),
        P(),
        P(),
        P(),
    )
    return jax.shard_map(
        per_device, mesh=mesh, in_specs=placed, out_specs=P(None, "chan", "tm"), check_vma=False
    )
```
